32 devices in a mesh: tm: 16 (over z, x, core), pairs: 2 (over y).
Axes of the slice: x: 2, y: 2, z: 4, core: 2. Of those that a mesh axis runs over, the one named last changes fastest.
Arguments:
- records: bfloat16 [2048, 65536], P('pairs', 'tm'), may hold values from -400 to 400
- station_order: int32 [2048], replicated, may hold values from 0 to 2047, each once
- block_list: int32 [20, 2], P('pairs'), may hold values from -1 to 31, as said below
Outputs:
- correlations: bfloat16 [20, 384, 2, 4096], P('pairs', 'tm')
The draws below stay inside these ranges and needn't reach their ends.
Inputs may be any that keep to these rules, and one draw needn't show every extreme that they name: `station_order`: each station once. `block_list`: rows k * 10 to (k + 1) * 10 - 1 belong to owner k of the pairs axis; an owner's live blocks come first and its other rows hold -1 in both columns; some owner has all 10 rows live; in a live row the second group is the first plus 0 to 3, modulo 32.
All inputs are finite; a program needn't handle non-finite values.
Results may differ from the reference program's by a relative error of at most 0.0076.
Values may be sent and summed in bfloat16 or wider, within the bound.
A program may use at most 192 MiB of HBM per device.

```python
import math
import jax
import jax.numpy as jnp
from jax import lax

RECEIVER_TOTAL = 2048
GSIZE = 64
GROUPS = 32
SUBWIN = 16
SAMPLES = 4096
TIME = 65536
BINS = 384
FIRST_BIN = 8
BAND = 64
HALF = 64
SLOTS = 10
N_PAIRS = 2


def draw_records(key, part):
    first, second, tertiary_item = jax.random.split(jax.random.fold_in(key, 11), 3)
    seismogram_pieces = TIME // 128
    base = jnp.clip(jax.random.normal(first, (RECEIVER_TOTAL, TIME), jnp.float32), -6.0, 6.0)
    gains = jnp.exp(jax.random.uniform(second, (RECEIVER_TOTAL, 1), jnp.float32, -1.2, 1.2))
    random_recordings = jnp.exp(jax.random.uniform(tertiary_item, (RECEIVER_TOTAL, seismogram_pieces), jnp.float32, -1.0, 1.0))
    averaged_amplitude_curve = jnp.repeat(random_recordings, 128, axis=1)
    return (base * gains * averaged_amplitude_curve).astype(jnp.bfloat16)


def draw_block_list(key, part):
    keys = jax.random.split(jax.random.fold_in(key, 23), 4)
    first = jax.random.randint(keys[0], (N_PAIRS, SLOTS), 0, GROUPS)
    offset = jax.random.randint(keys[1], (N_PAIRS, SLOTS), 0, 4)
    second = (first + offset) % GROUPS
    counts = jax.random.randint(keys[2], (N_PAIRS, 1), max(SLOTS // 8, 1), SLOTS // 2 + 1)
    largest_modulus = jax.random.randint(keys[3], (), 0, N_PAIRS)
    counts = jnp.where(jnp.arange(N_PAIRS)[:, None] == largest_modulus, SLOTS, counts)
    live = jnp.arange(SLOTS)[None, :] < counts
    first = jnp.where(live, first, -1)
    second = jnp.where(live, second, -1)
    return jnp.stack([first, second], axis=-1).reshape(N_PAIRS * SLOTS, 2).astype(jnp.int32)


def setup_inputs(seed: int = 0) -> dict:
    splits = jax.random.split(jax.random.key(seed), 4)
    records = draw_records(jax.random.fold_in(splits[3], 71), 0)
    station_order = jax.random.permutation(splits[1], RECEIVER_TOTAL).astype(jnp.int32)
    block_list = draw_block_list(jax.random.fold_in(splits[3], 71), 0)
    return {"records": records, "station_order": station_order, "block_list": block_list}


EPS = 1e-06

def dft_table(dtype):
    rows = jnp.arange(SAMPLES, dtype=jnp.int32)[:, None]
    cols = jnp.arange(BINS, dtype=jnp.int32)[None, :] + FIRST_BIN
    phase = (rows * cols % SAMPLES).astype(dtype) * (2.0 * math.pi / SAMPLES)
    return jnp.concatenate([jnp.cos(phase), -jnp.sin(phase)], axis=1).astype(jnp.bfloat16)

def window_sum(values, width):
    length = values.shape[1]
    out_len = length - width + 1
    total = jnp.zeros((values.shape[0], out_len), values.dtype)
    power = values
    size = 1
    offset = 0
    need = width
    while need > 0:
        if need % 2 == 1:
            total = total + power[:, offset:offset + out_len]
            offset = offset + size
        need = need // 2
        if need > 0:
            power = power[:, :-size] + power[:, size:]
            size = size * 2
    return total

def moving_norm(values, abs_padded, position):
    sums = window_sum(abs_padded, 2 * HALF + 1)
    upper = jnp.minimum(position + HALF, TIME - 1)
    lower = jnp.maximum(position - HALF, 0)
    counts = (upper - lower + 1).astype(abs_padded.dtype)
    return (values.astype(abs_padded.dtype) / (sums / counts + EPS)).astype(jnp.bfloat16)

def whiten(raw_rows):
    count = raw_rows.shape[0]
    parts = raw_rows.reshape(count, SUBWIN, 2, BINS // BAND, BAND)
    power = lax.optimization_barrier(jnp.mean(parts[:, :, 0] ** 2 + parts[:, :, 1] ** 2, axis=-1))
    level = jnp.sqrt(power + EPS)
    return (parts / level[:, :, None, :, None]).reshape(count, SUBWIN, 2, BINS).astype(jnp.bfloat16)

def reference(records, station_order, block_list):
    table = dft_table(jnp.float32)
    position = jnp.arange(TIME, dtype=jnp.int32)

    def per_group(block):
        magnitude = jnp.pad(jnp.abs(block.astype(jnp.float32)), ((0, 0), (HALF, HALF)))
        normed = moving_norm(block, magnitude, position)
        frames = normed.reshape(GSIZE * SUBWIN, SAMPLES)
        raw_rows = jnp.dot(frames, table, preferred_element_type=jnp.float32)
        return whiten(raw_rows.reshape(GSIZE, SUBWIN, 2 * BINS))
    fourier_coefficients = lax.map(per_group, records.reshape(RECEIVER_TOTAL // GSIZE, GSIZE, TIME))
    fourier_coefficients = jnp.transpose(fourier_coefficients.reshape(RECEIVER_TOTAL, SUBWIN, 2, BINS), (3, 1, 2, 0))
    group_members = station_order.reshape(GROUPS, GSIZE)

    def one_block(row):
        first = row[0]
        second = row[1]
        valid = (first >= 0).astype(jnp.float32)
        left = jnp.take(fourier_coefficients, group_members[jnp.maximum(first, 0)], axis=3).astype(jnp.float32)
        right = jnp.take(fourier_coefficients, group_members[jnp.maximum(second, 0)], axis=3).astype(jnp.float32)
        left_rows = left.reshape(BINS, SUBWIN * 2, GSIZE)
        right_rows = right.reshape(BINS, SUBWIN * 2, GSIZE)
        turned = jnp.stack([right[:, :, 1], -right[:, :, 0]], axis=2).reshape(BINS, SUBWIN * 2, GSIZE)
        cosine_component = jnp.einsum('fqi,fqj->fij', left_rows, right_rows)
        imag_part = jnp.einsum('fqi,fqj->fij', left_rows, turned)
        stacked = jnp.stack([cosine_component, imag_part], axis=1).reshape(BINS, 2, GSIZE * GSIZE)
        return (stacked * (valid / SUBWIN)).astype(jnp.bfloat16)
    return lax.map(one_block, block_list)
```

```python
import functools
import math

import jax
import jax.numpy as jnp
import numpy as np
from jax import lax
from jax.experimental import pallas as pl
from jax.experimental.pallas import tpu as pltpu
from jax.sharding import PartitionSpec as P

GSIZE = 64
SUBWIN = 16
SAMPLES = 4096
TIME = 65536
BINS = 384
FIRST_BIN = 8
BAND = 64
HALF = 64
EPS = 1e-06

EDGE = 128
TILE = 256
MIB = 1 << 20
MESH = pl.DeviceIdType.MESH


def table_rows(bins_each):
    bins = np.arange(BINS, dtype=np.int64) + FIRST_BIN
    phase = np.outer(bins, np.arange(SAMPLES, dtype=np.int64)) % SAMPLES * (2.0 * math.pi / SAMPLES)
    both = np.stack([np.cos(phase), -np.sin(phase)])
    both = both.reshape(2, BINS // bins_each, bins_each, SAMPLES).transpose(1, 0, 2, 3)
    return both.reshape(2 * BINS, SAMPLES).astype(np.float32).astype(jnp.bfloat16)


def band_matrix():
    source = np.arange(TILE + 2 * EDGE)[:, None] - EDGE
    target = np.arange(TILE)[None, :]
    return (np.abs(source - target) <= HALF).astype(np.float32).astype(jnp.bfloat16)


def spectra_kernel(bins_each, x_ref, left_ref, right_ref, inv_ref, band_ref, table_ref, out_ref, mag_ref, norm_ref):
    rows = x_ref.shape[0]
    mag_ref[:, :EDGE] = jnp.abs(left_ref[...])
    mag_ref[:, EDGE : EDGE + SAMPLES] = jnp.abs(x_ref[...])
    mag_ref[:, EDGE + SAMPLES :] = jnp.abs(right_ref[...])
    for n in range(SAMPLES // TILE):
        cols = slice(n * TILE, (n + 1) * TILE)
        sums = jnp.dot(
            mag_ref[:, n * TILE : (n + 1) * TILE + 2 * EDGE], band_ref[...], preferred_element_type=jnp.float32
        )
        level = sums * inv_ref[:, cols] + EPS
        scaled = x_ref[:, cols].astype(jnp.float32) * pl.reciprocal(level, approx=True)
        norm_ref[:, cols] = scaled.astype(jnp.bfloat16)
    raw = lax.dot_general(
        table_ref[...], norm_ref[...], (((1,), (1,)), ((), ())), preferred_element_type=jnp.float32
    )
    parts = raw.reshape(BINS // bins_each, 2, bins_each, rows)
    power = (parts[:, 0] * parts[:, 0] + parts[:, 1] * parts[:, 1]).reshape(BINS // BAND, BAND, rows)
    scale = lax.rsqrt(jnp.sum(power, axis=1, keepdims=True) * (1.0 / BAND) + EPS)
    scale = jnp.broadcast_to(scale, (BINS // BAND, BAND, rows)).reshape(BINS // bins_each, 1, bins_each, rows)
    out_ref[...] = (parts * scale).reshape(BINS // bins_each, 2 * bins_each, rows).astype(jnp.bfloat16)


def spectra(x, left, right, inv, bins_each):
    count = x.shape[0]
    rows = min(256, count)
    whole = lambda i: (0, 0)
    by_row = lambda i: (i, 0)
    return pl.pallas_call(
        functools.partial(spectra_kernel, bins_each),
        grid=(count // rows,),
        in_specs=[
            pl.BlockSpec((rows, SAMPLES), by_row),
            pl.BlockSpec((rows, EDGE), by_row),
            pl.BlockSpec((rows, EDGE), by_row),
            pl.BlockSpec((1, SAMPLES), whole),
            pl.BlockSpec((TILE + 2 * EDGE, TILE), whole),
            pl.BlockSpec((2 * BINS, SAMPLES), whole),
        ],
        out_specs=pl.BlockSpec((BINS // bins_each, 2 * bins_each, rows), lambda i: (0, 0, i)),
        out_shape=jax.ShapeDtypeStruct((BINS // bins_each, 2 * bins_each, count), jnp.bfloat16),
        scratch_shapes=[
            pltpu.VMEM((rows, SAMPLES + 2 * EDGE), jnp.bfloat16),
            pltpu.VMEM((rows, SAMPLES), jnp.bfloat16),
        ],
        compiler_params=pltpu.CompilerParams(vmem_limit_bytes=48 * MIB),
    )(x, left, right, inv, jnp.asarray(band_matrix()), jnp.asarray(table_rows(bins_each)))


def exchange_kernel(n, s_ref, x_ref, own_sem, send_sem, recv_sem, hop_send, hop_recv):
    t = lax.axis_index("tm")
    p = lax.axis_index("pairs")
    other = 1 - p
    barrier = pltpu.get_barrier_semaphore()
    for d in range(1, n):
        pl.semaphore_signal(barrier, inc=1, device_id=(lax.rem(t + d, n), p), device_id_type=MESH)
    pl.semaphore_signal(barrier, inc=1, device_id=(t, other), device_id_type=MESH)
    pl.semaphore_wait(barrier, n)

    own = pltpu.make_async_copy(s_ref.at[t], x_ref.at[p, t], own_sem)
    own.start()
    copies = []
    for d in range(1, n):
        to = lax.rem(t + d, n)
        copies.append(
            pltpu.make_async_remote_copy(
                src_ref=s_ref.at[to],
                dst_ref=x_ref.at[p, t],
                send_sem=send_sem.at[d],
                recv_sem=recv_sem.at[d],
                device_id=(to, p),
                device_id_type=MESH,
            )
        )
        copies[-1].start()
    hops = []
    for d in range(n):
        source = lax.rem(t + n - d, n)
        if d:
            copies[d - 1].wait_recv()
        hops.append(
            pltpu.make_async_remote_copy(
                src_ref=x_ref.at[p, source] if d else s_ref.at[t],
                dst_ref=x_ref.at[p, source],
                send_sem=hop_send.at[d],
                recv_sem=hop_recv.at[d],
                device_id=(t, other),
                device_id_type=MESH,
            )
        )
        hops[-1].start()
    own.wait()
    for copy in copies:
        copy.wait_send()
    for hop in hops:
        hop.wait()


def exchange(mine):
    n, rows, count = mine.shape
    return pl.pallas_call(
        functools.partial(exchange_kernel, n),
        out_shape=jax.ShapeDtypeStruct((2, n, rows, count), jnp.bfloat16),
        in_specs=[pl.BlockSpec(memory_space=pl.ANY)],
        out_specs=pl.BlockSpec(memory_space=pl.ANY),
        scratch_shapes=[
            pltpu.SemaphoreType.DMA,
            pltpu.SemaphoreType.DMA((n,)),
            pltpu.SemaphoreType.DMA((n,)),
            pltpu.SemaphoreType.DMA((n,)),
            pltpu.SemaphoreType.DMA((n,)),
        ],
        compiler_params=pltpu.CompilerParams(collective_id=0, has_side_effects=True),
    )(mine)


def pairs_kernel(bins, step, blocks_ref, left_ids, right_ids, x_ref, out_ref, y_ref):
    halves, rows, count = x_ref.shape
    ids = []
    for s in range(step):
        k = pl.program_id(0) * step + s
        a = blocks_ref[k, 0]
        b = blocks_ref[k, 1]
        live = a >= 0
        ids.append(jnp.where(live, left_ids[pl.ds(jnp.maximum(a, 0), 1), :], -1))
        ids.append(jnp.where(live, right_ids[pl.ds(jnp.maximum(b, 0), 1), :], -1))
    wanted = jnp.concatenate(ids, axis=1)
    station = lax.broadcasted_iota(jnp.int32, (count, step * 256), 0)
    total = None
    for h in range(halves):
        pick = jnp.where(station == wanted - h * count, 1.0, 0.0).astype(jnp.bfloat16)
        part = jnp.dot(x_ref[h], pick, preferred_element_type=jnp.float32)
        total = part if total is None else total + part
    for n in range(2 * step):
        y_ref[n] = total[:, n * 128 : (n + 1) * 128]
    lane = lax.broadcasted_iota(jnp.int32, (SUBWIN, 128), 1)
    straight = lane % 2 == 0
    low = lax.broadcasted_iota(jnp.int32, (GSIZE, 128), 1) < GSIZE
    for f in range(bins):
        for s in range(step):
            re_a = y_ref[2 * s, pl.ds(f, SUBWIN, stride=2 * bins), :]
            im_a = y_ref[2 * s, pl.ds(bins + f, SUBWIN, stride=2 * bins), :]
            re_b = y_ref[2 * s + 1, pl.ds(f, SUBWIN, stride=2 * bins), :]
            im_b = y_ref[2 * s + 1, pl.ds(bins + f, SUBWIN, stride=2 * bins), :]
            a_rows = jnp.concatenate(
                [jnp.where(straight, re_a, -im_a), jnp.where(straight, im_a, re_a)], axis=0
            ).astype(jnp.bfloat16)
            b_rows = jnp.concatenate([re_b, im_b], axis=0).astype(jnp.bfloat16)
            full = lax.dot_general(
                a_rows, b_rows, (((0,), (0,)), ((), ())), preferred_element_type=jnp.float32
            )
            kept = jnp.where(low, full[:GSIZE], full[GSIZE:]) * (1.0 / SUBWIN)
            out_ref[s, f] = kept.astype(jnp.bfloat16)


def correlate(x, station_order, block_list, bins):
    slots = block_list.shape[0]
    halves, rows, count = x.shape
    groups = station_order.reshape(-1, GSIZE)
    n_groups = groups.shape[0]
    left_ids = groups.reshape(n_groups, GSIZE // 2, 2).transpose(0, 2, 1)
    left_ids = jnp.repeat(left_ids.reshape(n_groups, GSIZE), 2, axis=1)
    right_ids = jnp.concatenate([groups, groups], axis=1)
    step = 2 if slots % 2 == 0 else 1
    out = pl.pallas_call(
        functools.partial(pairs_kernel, bins, step),
        grid_spec=pltpu.PrefetchScalarGridSpec(
            num_scalar_prefetch=1,
            grid=(slots // step,),
            in_specs=[
                pl.BlockSpec((n_groups, 128), lambda i, b: (0, 0)),
                pl.BlockSpec((n_groups, 128), lambda i, b: (0, 0)),
                pl.BlockSpec((halves, rows, count), lambda i, b: (0, 0, 0)),
            ],
            out_specs=pl.BlockSpec((step, bins, GSIZE, 128), lambda i, b: (i, 0, 0, 0)),
            scratch_shapes=[pltpu.VMEM((2 * step, rows, 128), jnp.float32)],
        ),
        out_shape=jax.ShapeDtypeStruct((slots, bins, GSIZE, 128), jnp.bfloat16),
        compiler_params=pltpu.CompilerParams(vmem_limit_bytes=48 * MIB),
    )(block_list, left_ids, right_ids, x)
    out = out.reshape(slots, bins, GSIZE // 2, 2, 128).transpose(0, 1, 3, 2, 4)
    return out.reshape(slots, bins, 2, GSIZE * GSIZE)


def local(records, station_order, block_list):
    n = lax.axis_size("tm")
    owners = lax.axis_size("pairs")
    share = SAMPLES // records.shape[1]
    x = records
    if share > 1:
        sets = [list(range(i, i + share)) for i in range(0, n, share)]
        x = lax.all_to_all(x, "tm", split_axis=0, concat_axis=1, axis_index_groups=sets, tiled=True)
    count = x.shape[0]
    left = lax.ppermute(x[:, -EDGE:], "tm", [(i, i + share) for i in range(n - share)])
    right = lax.ppermute(x[:, :EDGE], "tm", [(i + share, i) for i in range(n - share)])
    position = lax.axis_index("tm") // share * SAMPLES + jnp.arange(SAMPLES, dtype=jnp.int32)
    upper = jnp.minimum(position + HALF, TIME - 1)
    lower = jnp.maximum(position - HALF, 0)
    inv = (1.0 / (upper - lower + 1).astype(jnp.float32))[None, :]
    bins = BINS // n
    rows = SUBWIN * 2 * bins
    if share == 1 and owners == 2 and bins % 8 == 0:
        gathered = exchange(spectra(x, left, right, inv, bins)).reshape(owners, rows, count)
    else:
        mine = spectra(x, left, right, inv, BINS).reshape(2, n, bins, count)
        mine = lax.all_to_all(mine.transpose(1, 0, 2, 3), "tm", split_axis=0, concat_axis=0, tiled=True)
        mine = mine.reshape(SUBWIN, share, 2, bins, count).transpose(0, 2, 3, 1, 4)
        gathered = lax.all_gather(mine.reshape(rows, share * count), "pairs", axis=0)
    return correlate(gathered, station_order, block_list, bins)


def solution(mesh):
    placed = (P("pairs", "tm"), P(), P("pairs", None))
    return jax.shard_map(
        local, mesh=mesh, in_specs=placed, out_specs=P("pairs", "tm", None, None), check_vma=False
    )
```

```python
import functools
import math

import jax
import jax.numpy as jnp
import numpy as np
from jax import lax
from jax.experimental import pallas as pl
from jax.experimental.pallas import tpu as pltpu
from jax.sharding import PartitionSpec as P

GSIZE = 64
SUBWIN = 16
SAMPLES = 4096
TIME = 65536
BINS = 384
FIRST_BIN = 8
BAND = 64
HALF = 64
EPS = 1e-06

EDGE = 128
TILE = 256
MIB = 1 << 20
MESH = pl.DeviceIdType.MESH


def table_rows(bins_each):
    bins = np.arange(BINS, dtype=np.int64) + FIRST_BIN
    phase = np.outer(bins, np.arange(SAMPLES, dtype=np.int64)) % SAMPLES * (2.0 * math.pi / SAMPLES)
    both = np.stack([np.cos(phase), -np.sin(phase)])
    both = both.reshape(2, BINS // bins_each, bins_each, SAMPLES).transpose(1, 0, 2, 3)
    return both.reshape(2 * BINS, SAMPLES).astype(np.float32).astype(jnp.bfloat16)


def normalise(x_ref, norm_ref, mag_ref, band_ref, start):
    for n in range(SAMPLES // TILE):
        cols = slice(n * TILE, (n + 1) * TILE)
        sums = jnp.dot(
            mag_ref[:, n * TILE : (n + 1) * TILE + 2 * EDGE], band_ref[...], preferred_element_type=jnp.float32
        )
        position = start + n * TILE + lax.broadcasted_iota(jnp.int32, (1, TILE), 1)
        upper = jnp.minimum(position + HALF, TIME - 1)
        lower = jnp.maximum(position - HALF, 0)
        inv = 1.0 / (upper - lower + 1).astype(jnp.float32)
        scaled = x_ref[:, cols].astype(jnp.float32) * pl.reciprocal(sums * inv + EPS, approx=True)
        norm_ref[:, cols] = scaled.astype(jnp.bfloat16)


def fill_band(band_ref):
    source = lax.broadcasted_iota(jnp.int32, band_ref.shape, 0) - EDGE
    target = lax.broadcasted_iota(jnp.int32, band_ref.shape, 1)
    band_ref[...] = jnp.where(jnp.abs(source - target) <= HALF, 1.0, 0.0).astype(jnp.bfloat16)


def transform(table_ref, norm_ref, bins_each):
    rows = norm_ref.shape[0]
    raw = lax.dot_general(
        table_ref[...], norm_ref[...], (((1,), (1,)), ((), ())), preferred_element_type=jnp.float32
    )
    parts = raw.reshape(BINS // bins_each, 2, bins_each, rows)
    power = (parts[:, 0] * parts[:, 0] + parts[:, 1] * parts[:, 1]).reshape(BINS // BAND, BAND, rows)
    scale = lax.rsqrt(jnp.sum(power, axis=1, keepdims=True) * (1.0 / BAND) + EPS)
    scale = jnp.broadcast_to(scale, (BINS // BAND, BAND, rows)).reshape(BINS // bins_each, 1, bins_each, rows)
    return (parts * scale).reshape(BINS // bins_each, 2 * bins_each, rows).astype(jnp.bfloat16)


def spectra_kernel(share, x_ref, left_ref, right_ref, table_ref, out_ref, mag_ref, norm_ref, band_ref):
    @pl.when(pl.program_id(0) == 0)
    def _():
        fill_band(band_ref)

    mag_ref[:, :EDGE] = jnp.abs(left_ref[...])
    mag_ref[:, EDGE : EDGE + SAMPLES] = jnp.abs(x_ref[...])
    mag_ref[:, EDGE + SAMPLES :] = jnp.abs(right_ref[...])
    normalise(x_ref, norm_ref, mag_ref, band_ref, lax.div(lax.axis_index("tm"), share) * SAMPLES)
    out_ref[...] = transform(table_ref, norm_ref, BINS)


def spectra(x, left, right, share):
    count = x.shape[0]
    rows = min(256, count)
    whole = lambda i: (0, 0)
    by_row = lambda i: (i, 0)
    return pl.pallas_call(
        functools.partial(spectra_kernel, share),
        grid=(count // rows,),
        in_specs=[
            pl.BlockSpec((rows, SAMPLES), by_row),
            pl.BlockSpec((rows, EDGE), by_row),
            pl.BlockSpec((rows, EDGE), by_row),
            pl.BlockSpec((2 * BINS, SAMPLES), whole),
        ],
        out_specs=pl.BlockSpec((1, 2 * BINS, rows), lambda i: (0, 0, i)),
        out_shape=jax.ShapeDtypeStruct((1, 2 * BINS, count), jnp.bfloat16),
        scratch_shapes=[
            pltpu.VMEM((rows, SAMPLES + 2 * EDGE), jnp.bfloat16),
            pltpu.VMEM((rows, SAMPLES), jnp.bfloat16),
            pltpu.VMEM((TILE + 2 * EDGE, TILE), jnp.bfloat16),
        ],
        compiler_params=pltpu.CompilerParams(vmem_limit_bytes=48 * MIB),
    )(x, left, right, jnp.asarray(table_rows(BINS)))


def fused_kernel(n, bins, blocks, rec_ref, x_ref, table_hbm, got_ref, mag_ref, norm_ref, band_ref, table_ref,
                 left_ref, right_ref, mine_ref, table_sem, edge_send, edge_recv, own_sem, send_sem, recv_sem,
                 hop_send, hop_recv):
    t = lax.axis_index("tm")
    p = lax.axis_index("pairs")
    i = pl.program_id(0)
    rows = x_ref.shape[0]
    count = rows * blocks
    other = 1 - p
    after, before = lax.rem(t + 1, n), lax.rem(t + n - 1, n)
    table_copy = pltpu.make_async_copy(table_hbm, table_ref, table_sem)

    def columns(block):
        return pl.ds(pl.multiple_of(p * count + block * rows, 128), rows)

    def direct(block, d):
        to = lax.rem(t + d, n)
        return pltpu.make_async_remote_copy(
            src_ref=mine_ref.at[block, to],
            dst_ref=got_ref.at[t, :, columns(block)],
            send_sem=send_sem.at[block, d],
            recv_sem=recv_sem.at[block, d],
            device_id=(to, p),
            device_id_type=MESH,
        )

    def hop(block, d):
        source = lax.rem(t + n - d, n)
        return pltpu.make_async_remote_copy(
            src_ref=got_ref.at[source, :, columns(block)] if d else mine_ref.at[block, t],
            dst_ref=got_ref.at[source, :, columns(block)],
            send_sem=hop_send.at[block, d],
            recv_sem=hop_recv.at[block, d],
            device_id=(t, other),
            device_id_type=MESH,
        )

    def own(block):
        return pltpu.make_async_copy(mine_ref.at[block, t], got_ref.at[t, :, columns(block)], own_sem.at[block])

    def forward(block):
        for d in range(1, n):
            direct(block, d).wait_recv()
            hop(block, d).start()

    @pl.when(i == 0)
    def _():
        table_copy.start()
        barrier = pltpu.get_barrier_semaphore()
        for d in range(1, n):
            pl.semaphore_signal(barrier, inc=1, device_id=(lax.rem(t + d, n), p), device_id_type=MESH)
        pl.semaphore_signal(barrier, inc=1, device_id=(t, other), device_id_type=MESH)
        fill_band(band_ref)
        pl.semaphore_wait(barrier, n)
        edges = [
            pltpu.make_async_remote_copy(
                src_ref=rec_ref.at[:, pl.ds(first, EDGE)],
                dst_ref=landing,
                send_sem=edge_send.at[k],
                recv_sem=edge_recv.at[k],
                device_id=(to, p),
                device_id_type=MESH,
            )
            for k, (first, landing, to) in enumerate(
                [(SAMPLES - EDGE, left_ref, after), (0, right_ref, before)]
            )
        ]
        for edge in edges:
            edge.start()
        for edge in edges:
            edge.wait()

    at = pl.ds(pl.multiple_of(i * rows, rows), rows)
    left = jnp.abs(left_ref[at, :])
    right = jnp.abs(right_ref[at, :])
    mag_ref[:, :EDGE] = jnp.where(t == 0, jnp.zeros_like(left), left)
    mag_ref[:, EDGE : EDGE + SAMPLES] = jnp.abs(x_ref[...])
    mag_ref[:, EDGE + SAMPLES :] = jnp.where(t == n - 1, jnp.zeros_like(right), right)
    normalise(x_ref, norm_ref, mag_ref, band_ref, t * SAMPLES)

    @pl.when(i == 0)
    def _():
        table_copy.wait()

    mine_ref[i] = transform(table_ref, norm_ref, bins)
    for d in range(1, n):
        direct(i, d).start()
    hop(i, 0).start()
    own(i).start()

    @pl.when(i > 0)
    def _():
        forward(i - 1)

    @pl.when(i == blocks - 1)
    def _():
        forward(blocks - 1)

        def finish(block, carry):
            own(block).wait()
            for d in range(n):
                if d:
                    direct(block, d).wait_send()
                hop(block, d).wait()
            return carry

        lax.fori_loop(0, blocks, finish, 0)


def fused(records, n, bins):
    count = records.shape[0]
    rows = 256
    blocks = count // rows
    chunk = 2 * bins
    return pl.pallas_call(
        functools.partial(fused_kernel, n, bins, blocks),
        grid=(blocks,),
        in_specs=[
            pl.BlockSpec(memory_space=pl.ANY),
            pl.BlockSpec((rows, SAMPLES), lambda i: (i, 0)),
            pl.BlockSpec(memory_space=pl.ANY),
        ],
        out_specs=pl.BlockSpec(memory_space=pl.ANY),
        out_shape=jax.ShapeDtypeStruct((n, chunk, 2 * count), jnp.bfloat16),
        scratch_shapes=[
            pltpu.VMEM((rows, SAMPLES + 2 * EDGE), jnp.bfloat16),
            pltpu.VMEM((rows, SAMPLES), jnp.bfloat16),
            pltpu.VMEM((TILE + 2 * EDGE, TILE), jnp.bfloat16),
            pltpu.VMEM((2 * BINS, SAMPLES), jnp.bfloat16),
            pltpu.VMEM((count, EDGE), jnp.bfloat16),
            pltpu.VMEM((count, EDGE), jnp.bfloat16),
            pltpu.VMEM((blocks, n, chunk, rows), jnp.bfloat16),
            pltpu.SemaphoreType.DMA,
            pltpu.SemaphoreType.DMA((2,)),
            pltpu.SemaphoreType.DMA((2,)),
            pltpu.SemaphoreType.DMA((blocks,)),
            pltpu.SemaphoreType.DMA((blocks, n)),
            pltpu.SemaphoreType.DMA((blocks, n)),
            pltpu.SemaphoreType.DMA((blocks, n)),
            pltpu.SemaphoreType.DMA((blocks, n)),
        ],
        compiler_params=pltpu.CompilerParams(
            collective_id=0, has_side_effects=True, vmem_limit_bytes=48 * MIB
        ),
    )(records, records, jnp.asarray(table_rows(bins)))


def slot_ids(order_ref, group, live, lanes):
    group = jnp.maximum(group, 0)
    row = order_ref[pl.ds(group // 2, 1), :]
    high, low = lax.shift_right_logical(row, 5), lax.bitwise_and(row, 31)
    digits = jnp.where(lax.broadcasted_iota(jnp.int32, (16, 128), 0) == 0, high, low)
    member = lanes + (group % 2) * GSIZE
    pick = jnp.where(lax.broadcasted_iota(jnp.int32, (128, 128), 0) == member, 1.0, 0.0)
    moved = jnp.dot(
        digits.astype(jnp.float32).astype(jnp.bfloat16),
        pick.astype(jnp.bfloat16),
        preferred_element_type=jnp.float32,
    )
    ids = (moved[0:1] * 32.0 + moved[1:2]).astype(jnp.int32)
    return jnp.where(live, ids, -1)


def pairs_kernel(bins, step, blocks_ref, order_ref, x_ref, out_ref, y_ref):
    ids = []
    lane = lax.broadcasted_iota(jnp.int32, (1, 128), 1)
    left_lanes = lane % GSIZE // 2 * 2 + lane // GSIZE
    right_lanes = lane % GSIZE
    for s in range(step):
        k = pl.program_id(0) * step + s
        live = blocks_ref[k, 0] >= 0
        ids.append(slot_ids(order_ref, blocks_ref[k, 0], live, left_lanes))
        ids.append(slot_ids(order_ref, blocks_ref[k, 1], live, right_lanes))
    wanted = jnp.concatenate(ids, axis=1)
    station = lax.broadcasted_iota(jnp.int32, (x_ref.shape[1], step * 256), 0)
    pick = jnp.where(station == wanted, 1.0, 0.0).astype(jnp.bfloat16)
    total = jnp.dot(x_ref[...], pick, preferred_element_type=jnp.float32)
    for n in range(2 * step):
        y_ref[n] = total[:, n * 128 : (n + 1) * 128]
    lane = lax.broadcasted_iota(jnp.int32, (SUBWIN, 128), 1)
    straight = lane % 2 == 0
    low = lax.broadcasted_iota(jnp.int32, (GSIZE, 128), 1) < GSIZE
    for f in range(bins):
        for s in range(step):
            re_a = y_ref[2 * s, pl.ds(f, SUBWIN, stride=2 * bins), :]
            im_a = y_ref[2 * s, pl.ds(bins + f, SUBWIN, stride=2 * bins), :]
            re_b = y_ref[2 * s + 1, pl.ds(f, SUBWIN, stride=2 * bins), :]
            im_b = y_ref[2 * s + 1, pl.ds(bins + f, SUBWIN, stride=2 * bins), :]
            a_rows = jnp.concatenate(
                [jnp.where(straight, re_a, -im_a), jnp.where(straight, im_a, re_a)], axis=0
            ).astype(jnp.bfloat16)
            b_rows = jnp.concatenate([re_b, im_b], axis=0).astype(jnp.bfloat16)
            full = lax.dot_general(
                a_rows, b_rows, (((0,), (0,)), ((), ())), preferred_element_type=jnp.float32
            )
            kept = jnp.where(low, full[:GSIZE], full[GSIZE:]) * (1.0 / SUBWIN)
            out_ref[s, f] = kept.astype(jnp.bfloat16)


def correlate(x, station_order, block_list, bins):
    slots = block_list.shape[0]
    rows, stations = x.shape
    order = station_order.reshape(-1, 128)
    step = 2 if slots % 2 == 0 else 1
    out = pl.pallas_call(
        functools.partial(pairs_kernel, bins, step),
        grid_spec=pltpu.PrefetchScalarGridSpec(
            num_scalar_prefetch=1,
            grid=(slots // step,),
            in_specs=[
                pl.BlockSpec(order.shape, lambda i, b: (0, 0)),
                pl.BlockSpec((rows, stations), lambda i, b: (0, 0)),
            ],
            out_specs=pl.BlockSpec((step, bins, GSIZE, 128), lambda i, b: (i, 0, 0, 0)),
            scratch_shapes=[pltpu.VMEM((2 * step, rows, 128), jnp.float32)],
        ),
        out_shape=jax.ShapeDtypeStruct((slots, bins, GSIZE, 128), jnp.bfloat16),
        compiler_params=pltpu.CompilerParams(vmem_limit_bytes=48 * MIB),
    )(block_list, order, x)
    out = out.reshape(slots, bins, GSIZE // 2, 2, 128).transpose(0, 1, 3, 2, 4)
    return out.reshape(slots, bins, 2, GSIZE * GSIZE)


def local(records, station_order, block_list):
    n = lax.axis_size("tm")
    owners = lax.axis_size("pairs")
    share = SAMPLES // records.shape[1]
    bins = BINS // n
    rows = SUBWIN * 2 * bins
    if share == 1 and owners == 2 and bins % 8 == 0:
        return correlate(fused(records, n, bins).reshape(rows, -1), station_order, block_list, bins)
    x = records
    if share > 1:
        sets = [list(range(i, i + share)) for i in range(0, n, share)]
        x = lax.all_to_all(x, "tm", split_axis=0, concat_axis=1, axis_index_groups=sets, tiled=True)
    count = x.shape[0]
    left = lax.ppermute(x[:, -EDGE:], "tm", [(i, i + share) for i in range(n - share)])
    right = lax.ppermute(x[:, :EDGE], "tm", [(i + share, i) for i in range(n - share)])
    mine = spectra(x, left, right, share).reshape(2, n, bins, count)
    mine = lax.all_to_all(mine.transpose(1, 0, 2, 3), "tm", split_axis=0, concat_axis=0, tiled=True)
    mine = mine.reshape(SUBWIN, share, 2, bins, count).transpose(0, 2, 3, 1, 4)
    gathered = lax.all_gather(mine.reshape(rows, share * count), "pairs", axis=1, tiled=True)
    return correlate(gathered, station_order, block_list, bins)


def solution(mesh):
    placed = (P("pairs", "tm"), P(), P("pairs", None))
    return jax.shard_map(
        local, mesh=mesh, in_specs=placed, out_specs=P("pairs", "tm", None, None), check_vma=False
    )
```

```python
import functools
import math

import jax
import jax.numpy as jnp
import numpy as np
from jax import lax
from jax.experimental import pallas as pl
from jax.experimental.pallas import tpu as pltpu
from jax.sharding import PartitionSpec as P

GSIZE = 64
SUBWIN = 16
SAMPLES = 4096
TIME = 65536
BINS = 384
FIRST_BIN = 8
BAND = 64
HALF = 64
EPS = 1e-06

EDGE = 128
NEAR = 8
Z_SLOTS = 8
TILE = 256
MIB = 1 << 20
MESH = pl.DeviceIdType.MESH


def table_rows(bins_each):
    bins = np.arange(BINS, dtype=np.int64) + FIRST_BIN
    phase = np.outer(bins, np.arange(SAMPLES, dtype=np.int64)) % SAMPLES * (2.0 * math.pi / SAMPLES)
    both = np.stack([np.cos(phase), -np.sin(phase)])
    both = both.reshape(2, BINS // bins_each, bins_each, SAMPLES).transpose(1, 0, 2, 3)
    return both.reshape(2 * BINS, SAMPLES).astype(np.float32).astype(jnp.bfloat16)


def normalise(x_ref, norm_ref, mag_ref, band_ref, start, tiles):
    for n in tiles:
        cols = slice(n * TILE, (n + 1) * TILE)
        sums = jnp.dot(
            mag_ref[:, n * TILE : (n + 1) * TILE + 2 * EDGE], band_ref[...], preferred_element_type=jnp.float32
        )
        position = start + n * TILE + lax.broadcasted_iota(jnp.int32, (1, TILE), 1)
        upper = jnp.minimum(position + HALF, TIME - 1)
        lower = jnp.maximum(position - HALF, 0)
        inv = 1.0 / (upper - lower + 1).astype(jnp.float32)
        scaled = x_ref[:, cols].astype(jnp.float32) * pl.reciprocal(sums * inv + EPS, approx=True)
        norm_ref[:, cols] = scaled.astype(jnp.bfloat16)


def fill_band(band_ref):
    source = lax.broadcasted_iota(jnp.int32, band_ref.shape, 0) - EDGE
    target = lax.broadcasted_iota(jnp.int32, band_ref.shape, 1)
    band_ref[...] = jnp.where(jnp.abs(source - target) <= HALF, 1.0, 0.0).astype(jnp.bfloat16)


def transform(table_ref, norm_ref, bins_each):
    rows = norm_ref.shape[0]
    raw = lax.dot_general(
        table_ref[...], norm_ref[...], (((1,), (1,)), ((), ())), preferred_element_type=jnp.float32
    )
    parts = raw.reshape(BINS // bins_each, 2, bins_each, rows)
    power = (parts[:, 0] * parts[:, 0] + parts[:, 1] * parts[:, 1]).reshape(BINS // BAND, BAND, rows)
    scale = lax.rsqrt(jnp.sum(power, axis=1, keepdims=True) * (1.0 / BAND) + EPS)
    scale = jnp.broadcast_to(scale, (BINS // BAND, BAND, rows)).reshape(BINS // bins_each, 1, bins_each, rows)
    return (parts * scale).reshape(BINS // bins_each, 2 * bins_each, rows).astype(jnp.bfloat16)


def spectra_kernel(share, x_ref, left_ref, right_ref, table_ref, out_ref, mag_ref, norm_ref, band_ref):
    @pl.when(pl.program_id(0) == 0)
    def _():
        fill_band(band_ref)

    mag_ref[:, :EDGE] = jnp.abs(left_ref[...])
    mag_ref[:, EDGE : EDGE + SAMPLES] = jnp.abs(x_ref[...])
    mag_ref[:, EDGE + SAMPLES :] = jnp.abs(right_ref[...])
    normalise(x_ref, norm_ref, mag_ref, band_ref, lax.div(lax.axis_index("tm"), share) * SAMPLES, range(SAMPLES // TILE))
    out_ref[...] = transform(table_ref, norm_ref, BINS)


def spectra(x, left, right, share):
    count = x.shape[0]
    rows = min(256, count)
    whole = lambda i: (0, 0)
    by_row = lambda i: (i, 0)
    return pl.pallas_call(
        functools.partial(spectra_kernel, share),
        grid=(count // rows,),
        in_specs=[
            pl.BlockSpec((rows, SAMPLES), by_row),
            pl.BlockSpec((rows, EDGE), by_row),
            pl.BlockSpec((rows, EDGE), by_row),
            pl.BlockSpec((2 * BINS, SAMPLES), whole),
        ],
        out_specs=pl.BlockSpec((1, 2 * BINS, rows), lambda i: (0, 0, i)),
        out_shape=jax.ShapeDtypeStruct((1, 2 * BINS, count), jnp.bfloat16),
        scratch_shapes=[
            pltpu.VMEM((rows, SAMPLES + 2 * EDGE), jnp.bfloat16),
            pltpu.VMEM((rows, SAMPLES), jnp.bfloat16),
            pltpu.VMEM((TILE + 2 * EDGE, TILE), jnp.bfloat16),
        ],
        compiler_params=pltpu.CompilerParams(vmem_limit_bytes=48 * MIB),
    )(x, left, right, jnp.asarray(table_rows(BINS)))


def partner(t, d):
    for bit in (1, 2, 4, 8):
        if d & bit:
            t = t + bit * (1 - 2 * lax.rem(lax.div(t, bit), 2))
    return t


def fused_kernel(n, bins, blocks, rec_ref, x_ref, table_hbm, got_ref, mag_ref, norm_ref, band_ref, table_ref,
                 left_ref, right_ref, mine_ref, table_sem, edge_send, edge_recv, own_sem, send_sem, recv_sem,
                 hop_send, hop_recv):
    t = lax.axis_index("tm")
    p = lax.axis_index("pairs")
    i = pl.program_id(0)
    rows = x_ref.shape[0]
    count = rows * blocks
    other = 1 - p
    after, before = lax.rem(t + 1, n), lax.rem(t + n - 1, n)
    table_copy = pltpu.make_async_copy(table_hbm, table_ref, table_sem)
    partners = [partner(t, d) for d in range(n)]

    def columns(block):
        return pl.ds(pl.multiple_of(p * count + block * rows, 128), rows)

    def direct(block, d):
        to = partners[d]
        return pltpu.make_async_remote_copy(
            src_ref=mine_ref.at[block, to],
            dst_ref=got_ref.at[t, :, columns(block)],
            send_sem=send_sem.at[block, d],
            recv_sem=recv_sem.at[block, d],
            device_id=(to, p),
            device_id_type=MESH,
        )

    def across(block, d):
        to = partners[d]
        return pltpu.make_async_remote_copy(
            src_ref=mine_ref.at[block, to],
            dst_ref=got_ref.at[t, :, columns(block)],
            send_sem=hop_send.at[block, d],
            recv_sem=hop_recv.at[block, d],
            device_id=(to, other),
            device_id_type=MESH,
        )

    def hop(block, d):
        source = partners[d]
        return pltpu.make_async_remote_copy(
            src_ref=got_ref.at[source, :, columns(block)],
            dst_ref=got_ref.at[source, :, columns(block)],
            send_sem=hop_send.at[block, d],
            recv_sem=hop_recv.at[block, d],
            device_id=(t, other),
            device_id_type=MESH,
        )

    def own(block):
        return pltpu.make_async_copy(mine_ref.at[block, t], got_ref.at[t, :, columns(block)], own_sem.at[block])

    def forward(block):
        for d in range(NEAR, n):
            direct(block, d).wait_recv()
            hop(block, d).start()

    def edges():
        return [
            pltpu.make_async_remote_copy(
                src_ref=rec_ref.at[:, pl.ds(first, EDGE)],
                dst_ref=landing,
                send_sem=edge_send.at[k],
                recv_sem=edge_recv.at[k],
                device_id=(to, p),
                device_id_type=MESH,
            )
            for k, (first, landing, to) in enumerate(
                [(SAMPLES - EDGE, left_ref, after), (0, right_ref, before)]
            )
        ]

    @pl.when(i == 0)
    def _():
        table_copy.start()
        barrier = pltpu.get_barrier_semaphore()
        for d in range(1, n):
            pl.semaphore_signal(barrier, inc=1, device_id=(partners[d], p), device_id_type=MESH)
        for d in range(NEAR):
            pl.semaphore_signal(barrier, inc=1, device_id=(partners[d], other), device_id_type=MESH)
        fill_band(band_ref)
        pl.semaphore_wait(barrier, n - 1 + NEAR)
        for edge in edges():
            edge.start()

    mag_ref[:, EDGE : EDGE + SAMPLES] = jnp.abs(x_ref[...])
    last = SAMPLES // TILE - 1
    normalise(x_ref, norm_ref, mag_ref, band_ref, t * SAMPLES, range(1, last))

    @pl.when(i == 0)
    def _():
        for edge in edges():
            edge.wait()

    at = pl.ds(pl.multiple_of(i * rows, rows), rows)
    left = jnp.abs(left_ref[at, :])
    right = jnp.abs(right_ref[at, :])
    mag_ref[:, :EDGE] = jnp.where(t == 0, jnp.zeros_like(left), left)
    mag_ref[:, EDGE + SAMPLES :] = jnp.where(t == n - 1, jnp.zeros_like(right), right)
    normalise(x_ref, norm_ref, mag_ref, band_ref, t * SAMPLES, (0, last))

    @pl.when(i == 0)
    def _():
        table_copy.wait()

    mine_ref[i] = transform(table_ref, norm_ref, bins)
    for d in range(n - 1, 0, -1):
        direct(i, d).start()
        if d < NEAR:
            across(i, d).start()
    across(i, 0).start()
    own(i).start()

    @pl.when(i > 0)
    def _():
        forward(i - 1)

    @pl.when(i == blocks - 1)
    def _():
        forward(blocks - 1)

        def finish(block, carry):
            own(block).wait()
            for d in range(n):
                if d >= NEAR:
                    direct(block, d).wait_send()
                    hop(block, d).wait()
                else:
                    if d:
                        direct(block, d).wait()
                    across(block, d).wait()
            return carry

        lax.fori_loop(0, blocks, finish, 0)


def fused(records, n, bins):
    count = records.shape[0]
    rows = 256
    blocks = count // rows
    chunk = 2 * bins
    return pl.pallas_call(
        functools.partial(fused_kernel, n, bins, blocks),
        grid=(blocks,),
        in_specs=[
            pl.BlockSpec(memory_space=pl.ANY),
            pl.BlockSpec((rows, SAMPLES), lambda i: (i, 0)),
            pl.BlockSpec(memory_space=pl.ANY),
        ],
        out_specs=pl.BlockSpec(memory_space=pl.ANY),
        out_shape=jax.ShapeDtypeStruct((n, chunk, 2 * count), jnp.bfloat16),
        scratch_shapes=[
            pltpu.VMEM((rows, SAMPLES + 2 * EDGE), jnp.bfloat16),
            pltpu.VMEM((rows, SAMPLES), jnp.bfloat16),
            pltpu.VMEM((TILE + 2 * EDGE, TILE), jnp.bfloat16),
            pltpu.VMEM((2 * BINS, SAMPLES), jnp.bfloat16),
            pltpu.VMEM((count, EDGE), jnp.bfloat16),
            pltpu.VMEM((count, EDGE), jnp.bfloat16),
            pltpu.VMEM((blocks, n, chunk, rows), jnp.bfloat16),
            pltpu.SemaphoreType.DMA,
            pltpu.SemaphoreType.DMA((2,)),
            pltpu.SemaphoreType.DMA((2,)),
            pltpu.SemaphoreType.DMA((blocks,)),
            pltpu.SemaphoreType.DMA((blocks, n)),
            pltpu.SemaphoreType.DMA((blocks, n)),
            pltpu.SemaphoreType.DMA((blocks, n)),
            pltpu.SemaphoreType.DMA((blocks, n)),
        ],
        compiler_params=pltpu.CompilerParams(
            collective_id=0, has_side_effects=True, vmem_limit_bytes=48 * MIB
        ),
    )(records, records, jnp.asarray(table_rows(bins)))


def slot_ids(order_ref, group, live, lanes):
    group = jnp.maximum(group, 0)
    row = order_ref[pl.ds(group // 2, 1), :]
    high, low = lax.shift_right_logical(row, 5), lax.bitwise_and(row, 31)
    digits = jnp.where(lax.broadcasted_iota(jnp.int32, (16, 128), 0) == 0, high, low)
    member = lanes + (group % 2) * GSIZE
    pick = jnp.where(lax.broadcasted_iota(jnp.int32, (128, 128), 0) == member, 1.0, 0.0)
    moved = jnp.dot(
        digits.astype(jnp.float32).astype(jnp.bfloat16),
        pick.astype(jnp.bfloat16),
        preferred_element_type=jnp.float32,
    )
    ids = (moved[0:1] * 32.0 + moved[1:2]).astype(jnp.int32)
    return jnp.where(live, ids, -1)


def pairs_kernel(bins, step, blocks_ref, order_ref, x_ref, out_ref, y_ref, z_ref):
    ids = []
    lane = lax.broadcasted_iota(jnp.int32, (1, 128), 1)
    left_lanes = lane % (GSIZE // 2) * 2 + lane % GSIZE // (GSIZE // 2)
    right_lanes = lane % GSIZE
    for s in range(step):
        k = pl.program_id(0) * step + s
        live = blocks_ref[k, 0] >= 0
        left = slot_ids(order_ref, blocks_ref[k, 0], live, left_lanes)
        right = slot_ids(order_ref, blocks_ref[k, 1], live, right_lanes)
        ids.append(jnp.where(lane < GSIZE, left, right))
    wanted = jnp.concatenate(ids, axis=1)
    station = lax.broadcasted_iota(jnp.int32, (x_ref.shape[1], step * 128), 0)
    pick = jnp.where(station == wanted, 1.0, 0.0).astype(jnp.bfloat16)
    total = jnp.dot(x_ref[...], pick, preferred_element_type=jnp.float32)
    for n in range(step):
        y_ref[n] = total[:, n * 128 : (n + 1) * 128]
    half = GSIZE // 2
    low = lax.broadcasted_iota(jnp.int32, (SUBWIN, 128), 1) < GSIZE
    low_out = lax.broadcasted_iota(jnp.int32, (half, 128), 1) < GSIZE
    for f in range(bins):
        for s in range(step):
            re = y_ref[s, pl.ds(f, SUBWIN, stride=2 * bins), :]
            im = y_ref[s, pl.ds(bins + f, SUBWIN, stride=2 * bins), :]
            re_swap = pltpu.roll(re, GSIZE, 1)
            im_swap = pltpu.roll(im, GSIZE, 1)
            a_rows = jnp.concatenate([jnp.where(low, re, -im_swap), jnp.where(low, im, re_swap)], axis=0)
            b_rows = jnp.concatenate([jnp.where(low, re_swap, re), jnp.where(low, im_swap, im)], axis=0)
            full = lax.dot_general(
                a_rows.astype(jnp.bfloat16),
                b_rows.astype(jnp.bfloat16),
                (((0,), (0,)), ((), ())),
                preferred_element_type=jnp.float32,
            ) * (1.0 / SUBWIN)
            slot = (f * step + s) % Z_SLOTS
            for c in range(2):
                base = c * GSIZE
                kept = jnp.where(low_out, full[base : base + half], full[base + half : base + GSIZE])
                z_ref[slot, pl.ds(c, half, stride=2), :] = kept
            out_ref[s, f] = z_ref[slot].astype(jnp.bfloat16)


def correlate(x, station_order, block_list, bins):
    slots = block_list.shape[0]
    rows, stations = x.shape
    order = station_order.reshape(-1, 128)
    step = 2 if slots % 2 == 0 else 1
    out = pl.pallas_call(
        functools.partial(pairs_kernel, bins, step),
        grid_spec=pltpu.PrefetchScalarGridSpec(
            num_scalar_prefetch=1,
            grid=(slots // step,),
            in_specs=[
                pl.BlockSpec(order.shape, lambda i, b: (0, 0)),
                pl.BlockSpec((rows, stations), lambda i, b: (0, 0)),
            ],
            out_specs=pl.BlockSpec((step, bins, GSIZE, 128), lambda i, b: (i, 0, 0, 0)),
            scratch_shapes=[
                pltpu.VMEM((step, rows, 128), jnp.float32),
                pltpu.VMEM((Z_SLOTS, GSIZE, 128), jnp.float32),
            ],
        ),
        out_shape=jax.ShapeDtypeStruct((slots, bins, GSIZE, 128), jnp.bfloat16),
        compiler_params=pltpu.CompilerParams(vmem_limit_bytes=48 * MIB),
    )(block_list, order, x)
    out = out.reshape(slots, bins, GSIZE // 2, 2, 128).transpose(0, 1, 3, 2, 4)
    return out.reshape(slots, bins, 2, GSIZE * GSIZE)


def local(records, station_order, block_list):
    n = lax.axis_size("tm")
    owners = lax.axis_size("pairs")
    share = SAMPLES // records.shape[1]
    bins = BINS // n
    rows = SUBWIN * 2 * bins
    if share == 1 and owners == 2 and bins % 8 == 0:
        return correlate(fused(records, n, bins).reshape(rows, -1), station_order, block_list, bins)
    x = records
    if share > 1:
        sets = [list(range(i, i + share)) for i in range(0, n, share)]
        x = lax.all_to_all(x, "tm", split_axis=0, concat_axis=1, axis_index_groups=sets, tiled=True)
    count = x.shape[0]
    left = lax.ppermute(x[:, -EDGE:], "tm", [(i, i + share) for i in range(n - share)])
    right = lax.ppermute(x[:, :EDGE], "tm", [(i + share, i) for i in range(n - share)])
    mine = spectra(x, left, right, share).reshape(2, n, bins, count)
    mine = lax.all_to_all(mine.transpose(1, 0, 2, 3), "tm", split_axis=0, concat_axis=0, tiled=True)
    mine = mine.reshape(SUBWIN, share, 2, bins, count).transpose(0, 2, 3, 1, 4)
    gathered = lax.all_gather(mine.reshape(rows, share * count), "pairs", axis=1, tiled=True)
    return correlate(gathered, station_order, block_list, bins)


def solution(mesh):
    placed = (P("pairs", "tm"), P(), P("pairs", None))
    return jax.shard_map(
        local, mesh=mesh, in_specs=placed, out_specs=P("pairs", "tm", None, None), check_vma=False
    )
```

```python
import functools
import math

import jax
import jax.numpy as jnp
import numpy as np
from jax import lax
from jax.experimental import pallas as pl
from jax.experimental.pallas import tpu as pltpu
from jax.sharding import PartitionSpec as P

GSIZE = 64
SUBWIN = 16
SAMPLES = 4096
TIME = 65536
BINS = 384
FIRST_BIN = 8
BAND = 64
HALF = 64
EPS = 1e-06

EDGE = 128
NEAR = 8
TILE = 256
MIB = 1 << 20
MESH = pl.DeviceIdType.MESH


def table_rows(bins_each):
    bins = np.arange(BINS, dtype=np.int64) + FIRST_BIN
    phase = np.outer(bins, np.arange(SAMPLES, dtype=np.int64)) % SAMPLES * (2.0 * math.pi / SAMPLES)
    both = np.stack([np.cos(phase), -np.sin(phase)])
    both = both.reshape(2, BINS // bins_each, bins_each, SAMPLES).transpose(1, 0, 2, 3)
    return both.reshape(2 * BINS, SAMPLES).astype(np.float32).astype(jnp.bfloat16)


def normalise(x_ref, norm_ref, mag_ref, band_ref, start, tiles):
    for n in tiles:
        cols = slice(n * TILE, (n + 1) * TILE)
        sums = jnp.dot(
            mag_ref[:, n * TILE : (n + 1) * TILE + 2 * EDGE], band_ref[...], preferred_element_type=jnp.float32
        )
        position = start + n * TILE + lax.broadcasted_iota(jnp.int32, (1, TILE), 1)
        upper = jnp.minimum(position + HALF, TIME - 1)
        lower = jnp.maximum(position - HALF, 0)
        inv = 1.0 / (upper - lower + 1).astype(jnp.float32)
        scaled = x_ref[:, cols].astype(jnp.float32) * pl.reciprocal(sums * inv + EPS, approx=True)
        norm_ref[:, cols] = scaled.astype(jnp.bfloat16)


def fill_band(band_ref):
    source = lax.broadcasted_iota(jnp.int32, band_ref.shape, 0) - EDGE
    target = lax.broadcasted_iota(jnp.int32, band_ref.shape, 1)
    band_ref[...] = jnp.where(jnp.abs(source - target) <= HALF, 1.0, 0.0).astype(jnp.bfloat16)


def transform(table_ref, norm_ref, bins_each):
    rows = norm_ref.shape[0]
    raw = lax.dot_general(
        table_ref[...], norm_ref[...], (((1,), (1,)), ((), ())), preferred_element_type=jnp.float32
    )
    parts = raw.reshape(BINS // bins_each, 2, bins_each, rows)
    power = (parts[:, 0] * parts[:, 0] + parts[:, 1] * parts[:, 1]).reshape(BINS // BAND, BAND, rows)
    scale = lax.rsqrt(jnp.sum(power, axis=1, keepdims=True) * (1.0 / BAND) + EPS)
    scale = jnp.broadcast_to(scale, (BINS // BAND, BAND, rows)).reshape(BINS // bins_each, 1, bins_each, rows)
    return (parts * scale).reshape(BINS // bins_each, 2 * bins_each, rows).astype(jnp.bfloat16)


def spectra_kernel(share, x_ref, left_ref, right_ref, table_ref, out_ref, mag_ref, norm_ref, band_ref):
    @pl.when(pl.program_id(0) == 0)
    def _():
        fill_band(band_ref)

    mag_ref[:, :EDGE] = jnp.abs(left_ref[...])
    mag_ref[:, EDGE : EDGE + SAMPLES] = jnp.abs(x_ref[...])
    mag_ref[:, EDGE + SAMPLES :] = jnp.abs(right_ref[...])
    normalise(x_ref, norm_ref, mag_ref, band_ref, lax.div(lax.axis_index("tm"), share) * SAMPLES, range(SAMPLES // TILE))
    out_ref[...] = transform(table_ref, norm_ref, BINS)


def spectra(x, left, right, share):
    count = x.shape[0]
    rows = min(256, count)
    whole = lambda i: (0, 0)
    by_row = lambda i: (i, 0)
    return pl.pallas_call(
        functools.partial(spectra_kernel, share),
        grid=(count // rows,),
        in_specs=[
            pl.BlockSpec((rows, SAMPLES), by_row),
            pl.BlockSpec((rows, EDGE), by_row),
            pl.BlockSpec((rows, EDGE), by_row),
            pl.BlockSpec((2 * BINS, SAMPLES), whole),
        ],
        out_specs=pl.BlockSpec((1, 2 * BINS, rows), lambda i: (0, 0, i)),
        out_shape=jax.ShapeDtypeStruct((1, 2 * BINS, count), jnp.bfloat16),
        scratch_shapes=[
            pltpu.VMEM((rows, SAMPLES + 2 * EDGE), jnp.bfloat16),
            pltpu.VMEM((rows, SAMPLES), jnp.bfloat16),
            pltpu.VMEM((TILE + 2 * EDGE, TILE), jnp.bfloat16),
        ],
        compiler_params=pltpu.CompilerParams(vmem_limit_bytes=48 * MIB),
    )(x, left, right, jnp.asarray(table_rows(BINS)))


def partner(t, d):
    for bit in (1, 2, 4, 8):
        if d & bit:
            t = t + bit * (1 - 2 * lax.rem(lax.div(t, bit), 2))
    return t


def fused_kernel(n, bins, blocks, rec_ref, x_ref, table_hbm, got_ref, mag_ref, norm_ref, band_ref, table_ref,
                 left_ref, right_ref, mine_ref, table_sem, edge_send, edge_recv, own_sem, send_sem, recv_sem,
                 hop_send, hop_recv):
    t = lax.axis_index("tm")
    p = lax.axis_index("pairs")
    i = pl.program_id(0)
    rows = x_ref.shape[0]
    count = rows * blocks
    other = 1 - p
    after, before = lax.rem(t + 1, n), lax.rem(t + n - 1, n)
    table_copy = pltpu.make_async_copy(table_hbm, table_ref, table_sem)
    partners = [partner(t, d) for d in range(n)]

    def columns(block):
        return pl.ds(pl.multiple_of(p * count + block * rows, 128), rows)

    def direct(block, d):
        to = partners[d]
        return pltpu.make_async_remote_copy(
            src_ref=mine_ref.at[block, to],
            dst_ref=got_ref.at[t, :, columns(block)],
            send_sem=send_sem.at[block, d],
            recv_sem=recv_sem.at[block, d],
            device_id=(to, p),
            device_id_type=MESH,
        )

    def across(block, d):
        to = partners[d]
        return pltpu.make_async_remote_copy(
            src_ref=mine_ref.at[block, to],
            dst_ref=got_ref.at[t, :, columns(block)],
            send_sem=hop_send.at[block, d],
            recv_sem=hop_recv.at[block, d],
            device_id=(to, other),
            device_id_type=MESH,
        )

    def hop(block, d):
        source = partners[d]
        return pltpu.make_async_remote_copy(
            src_ref=got_ref.at[source, :, columns(block)],
            dst_ref=got_ref.at[source, :, columns(block)],
            send_sem=hop_send.at[block, d],
            recv_sem=hop_recv.at[block, d],
            device_id=(t, other),
            device_id_type=MESH,
        )

    def own(block):
        return pltpu.make_async_copy(mine_ref.at[block, t], got_ref.at[t, :, columns(block)], own_sem.at[block])

    def forward(block):
        for d in range(NEAR, n):
            direct(block, d).wait_recv()
            hop(block, d).start()

    def edges():
        return [
            pltpu.make_async_remote_copy(
                src_ref=rec_ref.at[:, pl.ds(first, EDGE)],
                dst_ref=landing,
                send_sem=edge_send.at[k],
                recv_sem=edge_recv.at[k],
                device_id=(to, p),
                device_id_type=MESH,
            )
            for k, (first, landing, to) in enumerate(
                [(SAMPLES - EDGE, left_ref, after), (0, right_ref, before)]
            )
        ]

    @pl.when(i == 0)
    def _():
        table_copy.start()
        barrier = pltpu.get_barrier_semaphore()
        for d in range(1, n):
            pl.semaphore_signal(barrier, inc=1, device_id=(partners[d], p), device_id_type=MESH)
        for d in range(NEAR):
            pl.semaphore_signal(barrier, inc=1, device_id=(partners[d], other), device_id_type=MESH)
        fill_band(band_ref)
        pl.semaphore_wait(barrier, n - 1 + NEAR)
        for edge in edges():
            edge.start()

    mag_ref[:, EDGE : EDGE + SAMPLES] = jnp.abs(x_ref[...])
    last = SAMPLES // TILE - 1
    normalise(x_ref, norm_ref, mag_ref, band_ref, t * SAMPLES, range(1, last))

    @pl.when(i == 0)
    def _():
        for edge in edges():
            edge.wait()

    at = pl.ds(pl.multiple_of(i * rows, rows), rows)
    left = jnp.abs(left_ref[at, :])
    right = jnp.abs(right_ref[at, :])
    mag_ref[:, :EDGE] = jnp.where(t == 0, jnp.zeros_like(left), left)
    mag_ref[:, EDGE + SAMPLES :] = jnp.where(t == n - 1, jnp.zeros_like(right), right)
    normalise(x_ref, norm_ref, mag_ref, band_ref, t * SAMPLES, (0, last))

    @pl.when(i == 0)
    def _():
        table_copy.wait()

    mine_ref[i] = transform(table_ref, norm_ref, bins)
    for d in range(n - 1, 0, -1):
        direct(i, d).start()
        if d < NEAR:
            across(i, d).start()
    across(i, 0).start()
    own(i).start()

    @pl.when(i > 1)
    def _():
        forward(i - 2)

    @pl.when(i == blocks - 1)
    def _():
        forward(blocks - 2)
        forward(blocks - 1)

        def finish(block, carry):
            own(block).wait()
            for d in range(n):
                if d >= NEAR:
                    direct(block, d).wait_send()
                    hop(block, d).wait()
                else:
                    if d:
                        direct(block, d).wait()
                    across(block, d).wait()
            return carry

        lax.fori_loop(0, blocks, finish, 0)


def fused(records, n, bins):
    count = records.shape[0]
    rows = 256
    blocks = count // rows
    chunk = 2 * bins
    return pl.pallas_call(
        functools.partial(fused_kernel, n, bins, blocks),
        grid=(blocks,),
        in_specs=[
            pl.BlockSpec(memory_space=pl.ANY),
            pl.BlockSpec((rows, SAMPLES), lambda i: (i, 0)),
            pl.BlockSpec(memory_space=pl.ANY),
        ],
        out_specs=pl.BlockSpec(memory_space=pl.ANY),
        out_shape=jax.ShapeDtypeStruct((n, chunk, 2 * count), jnp.bfloat16),
        scratch_shapes=[
            pltpu.VMEM((rows, SAMPLES + 2 * EDGE), jnp.bfloat16),
            pltpu.VMEM((rows, SAMPLES), jnp.bfloat16),
            pltpu.VMEM((TILE + 2 * EDGE, TILE), jnp.bfloat16),
            pltpu.VMEM((2 * BINS, SAMPLES), jnp.bfloat16),
            pltpu.VMEM((count, EDGE), jnp.bfloat16),
            pltpu.VMEM((count, EDGE), jnp.bfloat16),
            pltpu.VMEM((blocks, n, chunk, rows), jnp.bfloat16),
            pltpu.SemaphoreType.DMA,
            pltpu.SemaphoreType.DMA((2,)),
            pltpu.SemaphoreType.DMA((2,)),
            pltpu.SemaphoreType.DMA((blocks,)),
            pltpu.SemaphoreType.DMA((blocks, n)),
            pltpu.SemaphoreType.DMA((blocks, n)),
            pltpu.SemaphoreType.DMA((blocks, n)),
            pltpu.SemaphoreType.DMA((blocks, n)),
        ],
        compiler_params=pltpu.CompilerParams(
            collective_id=0, has_side_effects=True, vmem_limit_bytes=48 * MIB
        ),
    )(records, records, jnp.asarray(table_rows(bins)))


def slot_ids(order_ref, group, live, lanes):
    group = jnp.maximum(group, 0)
    row = order_ref[pl.ds(group // 2, 1), :]
    high, low = lax.shift_right_logical(row, 5), lax.bitwise_and(row, 31)
    digits = jnp.where(lax.broadcasted_iota(jnp.int32, (16, 128), 0) == 0, high, low)
    member = lanes + (group % 2) * GSIZE
    pick = jnp.where(lax.broadcasted_iota(jnp.int32, (128, 128), 0) == member, 1.0, 0.0)
    moved = jnp.dot(
        digits.astype(jnp.float32).astype(jnp.bfloat16),
        pick.astype(jnp.bfloat16),
        preferred_element_type=jnp.float32,
    )
    ids = (moved[0:1] * 32.0 + moved[1:2]).astype(jnp.int32)
    return jnp.where(live, ids, -1)


def pairs_kernel(bins, step, blocks_ref, order_ref, x_ref, out_ref, y_ref):
    ids = []
    lane = lax.broadcasted_iota(jnp.int32, (1, 128), 1)
    left_lanes = lane % GSIZE // 2 * 2 + lane // GSIZE
    right_lanes = lane % GSIZE
    for s in range(step):
        k = pl.program_id(0) * step + s
        live = blocks_ref[k, 0] >= 0
        ids.append(slot_ids(order_ref, blocks_ref[k, 0], live, left_lanes))
        ids.append(slot_ids(order_ref, blocks_ref[k, 1], live, right_lanes))
    wanted = jnp.concatenate(ids, axis=1)
    station = lax.broadcasted_iota(jnp.int32, (x_ref.shape[1], step * 256), 0)
    pick = jnp.where(station == wanted, 1.0, 0.0).astype(jnp.bfloat16)
    total = jnp.dot(x_ref[...], pick, preferred_element_type=jnp.float32)
    for n in range(2 * step):
        y_ref[n] = total[:, n * 128 : (n + 1) * 128]
    lane = lax.broadcasted_iota(jnp.int32, (SUBWIN, 128), 1)
    straight = lane % 2 == 0
    low = lax.broadcasted_iota(jnp.int32, (GSIZE, 128), 1) < GSIZE
    for f in range(bins):
        for s in range(step):
            re_a = y_ref[2 * s, pl.ds(f, SUBWIN, stride=2 * bins), :]
            im_a = y_ref[2 * s, pl.ds(bins + f, SUBWIN, stride=2 * bins), :]
            re_b = y_ref[2 * s + 1, pl.ds(f, SUBWIN, stride=2 * bins), :]
            im_b = y_ref[2 * s + 1, pl.ds(bins + f, SUBWIN, stride=2 * bins), :]
            a_rows = jnp.concatenate(
                [jnp.where(straight, re_a, -im_a), jnp.where(straight, im_a, re_a)], axis=0
            ).astype(jnp.bfloat16)
            b_rows = jnp.concatenate([re_b, im_b], axis=0).astype(jnp.bfloat16)
            full = lax.dot_general(
                a_rows, b_rows, (((0,), (0,)), ((), ())), preferred_element_type=jnp.float32
            )
            kept = jnp.where(low, full[:GSIZE], full[GSIZE:]) * (1.0 / SUBWIN)
            out_ref[s, f] = kept.astype(jnp.bfloat16)


def correlate(x, station_order, block_list, bins):
    slots = block_list.shape[0]
    rows, stations = x.shape
    order = station_order.reshape(-1, 128)
    step = 2 if slots % 2 == 0 else 1
    out = pl.pallas_call(
        functools.partial(pairs_kernel, bins, step),
        grid_spec=pltpu.PrefetchScalarGridSpec(
            num_scalar_prefetch=1,
            grid=(slots // step,),
            in_specs=[
                pl.BlockSpec(order.shape, lambda i, b: (0, 0)),
                pl.BlockSpec((rows, stations), lambda i, b: (0, 0)),
            ],
            out_specs=pl.BlockSpec((step, bins, GSIZE, 128), lambda i, b: (i, 0, 0, 0)),
            scratch_shapes=[pltpu.VMEM((2 * step, rows, 128), jnp.float32)],
        ),
        out_shape=jax.ShapeDtypeStruct((slots, bins, GSIZE, 128), jnp.bfloat16),
        compiler_params=pltpu.CompilerParams(vmem_limit_bytes=48 * MIB),
    )(block_list, order, x)
    out = out.reshape(slots, bins, GSIZE // 2, 2, 128).transpose(0, 1, 3, 2, 4)
    return out.reshape(slots, bins, 2, GSIZE * GSIZE)


def local(records, station_order, block_list):
    n = lax.axis_size("tm")
    owners = lax.axis_size("pairs")
    share = SAMPLES // records.shape[1]
    bins = BINS // n
    rows = SUBWIN * 2 * bins
    if share == 1 and owners == 2 and bins % 8 == 0:
        return correlate(fused(records, n, bins).reshape(rows, -1), station_order, block_list, bins)
    x = records
    if share > 1:
        sets = [list(range(i, i + share)) for i in range(0, n, share)]
        x = lax.all_to_all(x, "tm", split_axis=0, concat_axis=1, axis_index_groups=sets, tiled=True)
    count = x.shape[0]
    left = lax.ppermute(x[:, -EDGE:], "tm", [(i, i + share) for i in range(n - share)])
    right = lax.ppermute(x[:, :EDGE], "tm", [(i + share, i) for i in range(n - share)])
    mine = spectra(x, left, right, share).reshape(2, n, bins, count)
    mine = lax.all_to_all(mine.transpose(1, 0, 2, 3), "tm", split_axis=0, concat_axis=0, tiled=True)
    mine = mine.reshape(SUBWIN, share, 2, bins, count).transpose(0, 2, 3, 1, 4)
    gathered = lax.all_gather(mine.reshape(rows, share * count), "pairs", axis=1, tiled=True)
    return correlate(gathered, station_order, block_list, bins)


def solution(mesh):
    placed = (P("pairs", "tm"), P(), P("pairs", None))
    return jax.shard_map(
        local, mesh=mesh, in_specs=placed, out_specs=P("pairs", "tm", None, None), check_vma=False
    )
```
